32 devices in a mesh: ep: 2 (over x), kv: 16 (over z, y, core).
Axes of the slice: x: 2, y: 2, z: 4, core: 2. Of those that a mesh axis runs over, the one named last changes fastest.
Arguments:
- queries: bfloat16 [32, 1536], P(('ep', 'kv'))
- key_cache_pages: bfloat16 [512, 64, 512], P(('ep', 'kv'))
- value_cache_pages: bfloat16 [512, 64, 512], P(('ep', 'kv')), may hold values from -5 to 5
- page_table: int32 [32, 65], replicated, may hold values from 0 to 511, as said below
- lengths: int32 [32], replicated, may hold values from 2 to 32768, as said below
- sink_head_logits: float32 [24], replicated, may hold values from -1 to 5
- output_weight: bfloat16 [1536, 1536], replicated, may hold values from -0.15625 to 0.15625
- decode_stream: bfloat16 [32, 1536], P(('ep', 'kv')), may hold values from -6 to 6
- prefill_stream: bfloat16 [4064, 1536], P(('ep', 'kv')), may hold values from -6 to 6
- norm_gain: float32 [1536], replicated, may hold values from 0.1 to 1.9
- expert_gate: bfloat16 [16, 1536, 512], P('kv'), may hold values from -0.15625 to 0.15625
- expert_up: bfloat16 [16, 1536, 512], P('kv'), may hold values from -0.15625 to 0.15625
- expert_down: bfloat16 [16, 512, 1536], P('kv'), may hold values from -0.25 to 0.25
- route_ids: int32 [4096, 8], P(('ep', 'kv')), may hold values from 0 to 15, all different within a row; in each aligned block of 128 rows (0 to 127, 128 to 255, ...) at most 96 rows name the same one
- route_gates: float32 [4096, 8], P(('ep', 'kv')), may hold values from 0.03 to 0.6
Outputs:
- layer_out: bfloat16 [4096, 1536], P(('ep', 'kv'))
The draws below stay inside these ranges and needn't reach their ends.
Inputs may be any that keep to these rules, and one draw needn't show every extreme that they name: In each aligned block of 16 requests, 1 request, which ones drawn from the seed, have lengths of 4096 or more; the others have lengths of at most 512. `page_table`: no two live slots name the same page. Every slot of a request in aligned block g of 16 requests names a page among g * 16 * 16 to (g + 1) * 16 * 16 - 1. `route_ids`: every row names 8 different experts; among the 128 rows of one device no expert is named by more than 96 rows.
All inputs are finite; a program needn't handle non-finite values.
Results may differ from the reference program's by a relative error of at most 0.0053.
Values may be sent and summed in bfloat16 or wider, within the bound.
A program may use at most 128 MiB of HBM per device.

```python
import math
import jax
import jax.numpy as jnp
import numpy as np
from jax import lax

D = 1536
QUERY_HEADS = 24
KEY_VALUE_HEADS = 8
HEAD_WIDTH = 64
FF = 512
EXPERTS = 16
TOPK = 8
WINDOW = 4096
PAGE_POSITIONS = 64
WINDOW_SLOTS = 65
MAXLEN = 32768
SHORT = 512
POOL_DEV = 16
LONG_GROUP = 1
ROWS_DEV = 128
PRE_DEV = 127
CAP = 96
REQS = 32
PAGE_TOTAL = 512
TOKENS = 4096
PREFILL = 4064
N_EP = 2
N_KV = 16


def layout_tables(key):
    layout_key = jax.random.fold_in(key, 7)
    pick_key, long_key, short_key, pool_key = jax.random.split(layout_key, 4)
    request_index = jnp.arange(REQS, dtype=jnp.int32)
    group_of = request_index // N_KV
    shuffled = jax.random.permutation(pick_key, REQS).astype(jnp.int32)
    sort_order = jnp.argsort(group_of * REQS + shuffled, stable=True).astype(jnp.int32)
    position_of = jnp.zeros((REQS,), jnp.int32).at[sort_order].set(request_index)
    group_rank = position_of - group_of * N_KV
    is_long = (group_rank < LONG_GROUP).astype(jnp.int32)
    request_order = jnp.argsort(group_rank * N_EP + group_of, stable=True).astype(jnp.int32)
    long_length = jax.random.randint(long_key, (REQS,), WINDOW, MAXLEN + 1, dtype=jnp.int32)
    short_length = jax.random.randint(short_key, (REQS,), 2, SHORT + 1, dtype=jnp.int32)
    lengths = jnp.where(is_long == 1, long_length, short_length)
    lengths = lengths.at[request_order[0]].set(MAXLEN).at[request_order[LONG_GROUP * N_EP]].set(2)
    first_page = jnp.maximum(lengths - WINDOW, 0) // PAGE_POSITIONS
    slot_index = jnp.arange(WINDOW_SLOTS, dtype=jnp.int32)
    live_slot = ((first_page[:, None] + slot_index[None, :]) * PAGE_POSITIONS < lengths[:, None]).astype(jnp.int32)
    live_grouped = live_slot.reshape(N_EP, N_KV * WINDOW_SLOTS)
    dead_grouped = 1 - live_grouped
    live_rank = jnp.cumsum(live_grouped, axis=1) - live_grouped
    dead_rank = jnp.cumsum(dead_grouped, axis=1) - dead_grouped
    group_pool = N_KV * POOL_DEV
    live_total = jnp.sum(live_grouped, axis=1, keepdims=True)
    spare_count = jnp.maximum(group_pool - live_total, 1)
    chosen = jnp.where(live_grouped == 1, live_rank, jnp.minimum(live_total + dead_rank % spare_count, group_pool - 1))
    pool_scores = jax.random.randint(pool_key, (N_EP, group_pool), 0, 4096, dtype=jnp.int32) * group_pool + jnp.arange(group_pool, dtype=jnp.int32)[None, :]
    pool_order = jnp.argsort(pool_scores, axis=1, stable=True).astype(jnp.int32)
    picked = jnp.take_along_axis(pool_order, chosen, axis=1)
    group_base = (jnp.arange(N_EP, dtype=jnp.int32) * group_pool)[:, None]
    page_map = (picked + group_base).reshape(REQS, WINDOW_SLOTS)
    return (lengths, page_map)


def draw_lengths(key, part):
    return layout_tables(key)[0]


def draw_page_table(key, part):
    return layout_tables(key)[1]


def drawn_pairs(key):
    key_value_pair = jnp.clip(jax.random.normal(jax.random.fold_in(key, 13), (PAGE_TOTAL, PAGE_POSITIONS, KEY_VALUE_HEADS * HEAD_WIDTH), jnp.float32), -5.0, 5.0)
    query_values = jnp.clip(jax.random.normal(jax.random.fold_in(key, 17), (REQS, QUERY_HEADS * HEAD_WIDTH), jnp.float32), -5.0, 5.0)
    return (key_value_pair, query_values)


def draw_key_cache_pages(key, part):
    return drawn_pairs(key)[0].astype(jnp.bfloat16)


def draw_queries(key, part):
    return drawn_pairs(key)[1].astype(jnp.bfloat16)


def block_scale(own_key, shape, shards, low, high):
    gain = 1.0
    for position, parts in shards:
        draws = jax.random.uniform(jax.random.fold_in(jax.random.fold_in(own_key, 6), position), (parts,), jnp.float32, low / len(shards), high / len(shards))
        gain = gain * jnp.repeat(jnp.exp(draws), shape[position] // parts).reshape((-1,) + (1,) * (len(shape) - 1 - position))
    return gain


def routed_block(rng, own, number, rows, count, top, limit, skew):
    ranking = jax.random.permutation(rng, count)
    packed, common = portions_of(count, rows * top, limit, skew, True), portions_of(count, rows * top, limit, skew, False)
    places = jnp.arange(count)

    def named(sizes, offset_by):
        used = int((sizes > 0).sum())
        fixed = max(1, used // 4)
        moved = fixed + (places - fixed + offset_by * (used - fixed)) % max(1, count - fixed)
        return jnp.zeros((count,), jnp.int32).at[ranking[jnp.where(places < fixed, places, moved)]].set(jnp.asarray(sizes, jnp.int32))

    sizes = jnp.where(number % 4 == 0, named(packed, number // 4), named(common, number - number // 4 - 1))
    mixed = jax.random.permutation(jax.random.fold_in(own, 3), count)
    source_of, sink = mixed[0:count // 2 * 2:2], mixed[1:count // 2 * 2:2]
    room = jnp.minimum(sizes[source_of] - 1, limit - sizes[sink]) // 2
    room = jnp.where((source_of == ranking[0]) | (sink == ranking[0]) | (sizes[sink] == 0), 0, jnp.maximum(room, 0))
    moved = jax.random.randint(jax.random.fold_in(own, 4), (count // 2,), 0, 1 << 20) % (room + 1)
    sizes = sizes.at[source_of].add(-moved).at[sink].add(moved)
    items = jnp.searchsorted(jnp.cumsum(sizes), jnp.arange(rows * top), side="right").astype(jnp.int32)
    grid = items.reshape(top, rows).T
    grid = grid[jax.random.permutation(jax.random.fold_in(own, 1), rows)]
    offset_by = jax.random.randint(jax.random.fold_in(own, 2), (rows, 1), 0, top)
    return jnp.take_along_axis(grid, (jnp.arange(top)[None, :] + offset_by) % top, axis=1)


def portions_of(number_of, total, limit, lean, full):
    weights = [(1 << 20) // math.isqrt(grade ** lean) + 1 for grade in range(1, number_of + 1)]
    largest = limit if full else min(limit, max(-(-total // number_of), total * weights[0] // sum(weights)))
    least = 1 if total - largest >= number_of - 1 else 0
    counts, surplus = [largest] + [least] * (number_of - 1), total - largest - least * (number_of - 1)
    while surplus > 0:
        candidates = [i for i in range(1, number_of) if counts[i] < largest] or [i for i in range(1, number_of) if counts[i] < limit]
        pool, remaining = sum([weights[i] for i in candidates]), surplus
        for i in candidates:
            extra = min(limit - counts[i], max(1, remaining * weights[i] // pool), surplus)
            counts[i] = counts[i] + extra
            surplus = surplus - extra
    return np.array(counts)


def noise(own_key, shape, scale, bound, shards=(), kind=jnp.bfloat16):
    gain = block_scale(own_key, shape, shards, -0.22, 0.18) if shards else 1.0
    values = jax.random.normal(own_key, shape, jnp.float32) * scale * gain
    return jnp.minimum(jnp.maximum(values, -bound), bound).astype(kind)


def setup_inputs(seed: int = 0) -> dict:
    splits = jax.random.split(jax.random.key(seed), 16)
    queries = draw_queries(jax.random.fold_in(splits[15], 71), 0)
    key_cache_pages = draw_key_cache_pages(jax.random.fold_in(splits[15], 71), 0)
    value_cache_pages = noise(splits[2], (PAGE_TOTAL, PAGE_POSITIONS, KEY_VALUE_HEADS * HEAD_WIDTH), 1.0, 5.0, ((0, 32),))
    page_table = draw_page_table(jax.random.fold_in(splits[15], 71), 0)
    lengths = draw_lengths(jax.random.fold_in(splits[15], 71), 0)
    sink_head_logits = jnp.clip(jax.random.uniform(splits[5], (QUERY_HEADS,), jnp.float32, -1.0, 5.0), -1.0, 5.0)
    output_weight = noise(splits[6], (QUERY_HEADS * HEAD_WIDTH, D), (QUERY_HEADS * HEAD_WIDTH) ** -0.5, 0.15625)
    decode_stream = noise(splits[7], (REQS, D), 1.0, 6.0, ((0, 32),))
    prefill_stream = noise(splits[8], (PREFILL, D), 1.0, 6.0, ((0, 32),))
    norm_gain = jnp.clip(1.0 + 0.18 * jax.random.normal(splits[9], (D,), jnp.float32), 0.1, 1.9)
    expert_gate = noise(splits[10], (EXPERTS, D, FF), D ** -0.5, 0.15625, ((0, 16),))
    expert_up = noise(splits[11], (EXPERTS, D, FF), D ** -0.5, 0.15625, ((0, 16),))
    expert_down = noise(splits[12], (EXPERTS, FF, D), FF ** -0.5, 0.25, ((0, 16),))
    route_ids_keys = jax.random.split(jax.random.fold_in(splits[13], 1), TOKENS // ROWS_DEV)
    route_ids_turns = jax.random.permutation(jax.random.fold_in(splits[13], 3), TOKENS // ROWS_DEV)
    route_ids = jax.vmap(lambda own, number: routed_block(jax.random.fold_in(splits[13], 2), own, number, ROWS_DEV, EXPERTS, TOPK, CAP, 2))(route_ids_keys, route_ids_turns).reshape((TOKENS, TOPK))
    route_gates = jnp.clip(jnp.exp(math.log(0.6) - 2.9957323 * jax.random.uniform(splits[14], (TOKENS, TOPK), jnp.float32) ** block_scale(splits[14], (TOKENS, TOPK), ((0, 32),), -0.2, 0.2)), 0.03, 0.6)
    return {"queries": queries, "key_cache_pages": key_cache_pages, "value_cache_pages": value_cache_pages, "page_table": page_table, "lengths": lengths, "sink_head_logits": sink_head_logits, "output_weight": output_weight, "decode_stream": decode_stream, "prefill_stream": prefill_stream, "norm_gain": norm_gain, "expert_gate": expert_gate, "expert_up": expert_up, "expert_down": expert_down, "route_ids": route_ids, "route_gates": route_gates}


lowest = -1e+30

def reference(queries, key_cache_pages, value_cache_pages, page_table, lengths, sink_head_logits, output_weight, decode_stream, prefill_stream, norm_gain, expert_gate, expert_up, expert_down, route_ids, route_gates):
    group_width = QUERY_HEADS // KEY_VALUE_HEADS
    score_scale = HEAD_WIDTH ** (-0.5)
    window_start = jnp.maximum(lengths - WINDOW, 0)
    first_page = window_start // PAGE_POSITIONS
    slot_index = jnp.arange(WINDOW_SLOTS, dtype=jnp.int32)
    page_offsets = jnp.arange(PAGE_POSITIONS, dtype=jnp.int32)

    def per_request(inputs):
        single_query_row, page_table_row, length, window_begin, first_slot = inputs
        keys_of_page = key_cache_pages[page_table_row].reshape(WINDOW_SLOTS, PAGE_POSITIONS, KEY_VALUE_HEADS, HEAD_WIDTH).astype(jnp.float32)
        values_of_page = value_cache_pages[page_table_row].reshape(WINDOW_SLOTS, PAGE_POSITIONS, KEY_VALUE_HEADS, HEAD_WIDTH).astype(jnp.float32)
        positions = (first_slot + slot_index)[:, None] * PAGE_POSITIONS + page_offsets[None, :]
        in_window = (positions >= window_begin) & (positions < length)
        grouped_queries = single_query_row.reshape(KEY_VALUE_HEADS, group_width, HEAD_WIDTH).astype(jnp.float32)
        scores = jnp.einsum('gqd,ptgd->pgqt', grouped_queries, keys_of_page) * score_scale
        mask_full = in_window[:, None, None, :]
        scores = jnp.where(mask_full, scores, lowest)
        slot_max = lax.optimization_barrier(jnp.max(scores, axis=-1))
        weights = jnp.where(mask_full, jnp.exp(scores - slot_max[..., None]), 0.0).astype(jnp.bfloat16)
        weights_wide = weights.astype(jnp.float32)
        slot_total = lax.optimization_barrier(jnp.sum(weights_wide, axis=-1))
        slot_out = jnp.einsum('pgqt,ptgd->pgqd', weights_wide, values_of_page)
        live_slot = jnp.any(in_window, axis=-1)[:, None, None]
        slot_max = jnp.where(live_slot, slot_max, lowest)
        request_max = lax.optimization_barrier(jnp.max(slot_max, axis=0))
        rescale = jnp.where(live_slot, jnp.exp(slot_max - request_max[None]), 0.0)
        request_total = lax.optimization_barrier(jnp.sum(rescale * slot_total, axis=0))
        request_out = lax.optimization_barrier(jnp.sum(rescale[..., None] * slot_out, axis=0))
        sink_logit_row = sink_head_logits.reshape(KEY_VALUE_HEADS, group_width)
        ceiling = jnp.maximum(request_max, sink_logit_row)
        factor = jnp.exp(request_max - ceiling)
        attended = request_out * factor[..., None] / (request_total * factor + jnp.exp(sink_logit_row - ceiling))[..., None]
        return attended.reshape(QUERY_HEADS * HEAD_WIDTH).astype(jnp.bfloat16)
    attended = lax.map(per_request, (queries, page_table, lengths, window_start, first_page))
    decode_hidden = (decode_stream.astype(jnp.float32) + jnp.dot(attended, output_weight, preferred_element_type=jnp.float32)).astype(jnp.bfloat16)
    mixed_rows = jnp.concatenate([prefill_stream.reshape(REQS, PRE_DEV, D), decode_hidden.reshape(REQS, 1, D)], axis=1).reshape(TOKENS, D)
    residual = mixed_rows.astype(jnp.float32)
    normed = (residual * lax.rsqrt(lax.optimization_barrier(jnp.mean(residual * residual, axis=-1, keepdims=True)) + 1e-06) * norm_gain.astype(jnp.float32)).astype(jnp.bfloat16)
    pair_count = TOKENS * TOPK
    pair_expert = route_ids.reshape(-1).astype(jnp.int32)
    pair_order = jnp.argsort(pair_expert, stable=True).astype(jnp.int32)
    expert_index = jnp.arange(EXPERTS, dtype=jnp.int32)
    expert_hits = lax.optimization_barrier(jnp.sum((pair_expert[:, None] == expert_index[None, :]).astype(jnp.int32), axis=0))
    block_rows = 512
    padded = (expert_hits + block_rows - 1) // block_rows * block_rows
    group_begin = jnp.cumsum(padded) - padded
    group_end = group_begin + padded
    hit_begin = jnp.cumsum(expert_hits) - expert_hits
    sorted_expert = pair_expert[pair_order]
    sorted_rank = jnp.arange(pair_count, dtype=jnp.int32) - hit_begin[sorted_expert]
    sorted_slot = group_begin[sorted_expert] + sorted_rank
    block_count = (pair_count + block_rows - 1) // block_rows + EXPERTS
    slot_pair = jnp.full((block_count * block_rows,), pair_count, jnp.int32).at[sorted_slot].set(pair_order)
    block_first = jnp.arange(block_count, dtype=jnp.int32) * block_rows
    block_expert = jnp.minimum(lax.optimization_barrier(jnp.sum((group_end[None, :] <= block_first[:, None]).astype(jnp.int32), axis=1)), EXPERTS - 1).astype(jnp.int32)
    slot_token = jnp.where(slot_pair < pair_count, slot_pair // TOPK, TOKENS).astype(jnp.int32)
    gate_flat = jnp.concatenate([route_gates.reshape(-1).astype(jnp.float32), jnp.zeros((1,), jnp.float32)])
    slot_gate = gate_flat[slot_pair]
    extended = jnp.concatenate([normed, jnp.zeros((1, D), jnp.bfloat16)], axis=0)

    def expert_step(accum, inputs):
        token_block, gate_block, expert = inputs
        rows_in = extended[token_block]
        gate_part = jnp.dot(rows_in, expert_gate[expert], preferred_element_type=jnp.float32)
        up_part = jnp.dot(rows_in, expert_up[expert], preferred_element_type=jnp.float32)
        hidden = (jax.nn.silu(gate_part) * up_part).astype(jnp.bfloat16)
        produced = jnp.dot(hidden, expert_down[expert], preferred_element_type=jnp.float32).astype(jnp.bfloat16)
        accum = accum.at[token_block].add(produced.astype(jnp.float32) * gate_block[:, None])
        return (accum, None)
    accum = jnp.zeros((TOKENS + 1, D), jnp.float32)
    accum, _ = lax.scan(expert_step, accum, (slot_token.reshape(block_count, block_rows), slot_gate.reshape(block_count, block_rows), block_expert))
    return (residual + accum[:TOKENS]).astype(jnp.bfloat16)
```

```python
import functools

import jax
import jax.numpy as jnp
from jax import lax
from jax.experimental import pallas as pl
from jax.experimental.pallas import tpu as pltpu
from jax.sharding import PartitionSpec as P

QUERY_HEADS = 24
KEY_VALUE_HEADS = 8
HEAD_WIDTH = 64
TOPK = 8
WINDOW = 4096
LANES = 128
HEAD_ROWS = 32

lowest = -1e30
MESH = pl.DeviceIdType.MESH


def silu_times(gate_part, up_part):
    return (gate_part / (1.0 + jnp.exp(-gate_part)) * up_part).astype(jnp.bfloat16)


def kernel(
    n,
    query_ref,
    bias_ref,
    sink_ref,
    decode_ref,
    prefill_ref,
    gain_ref,
    ids_ref,
    gates_ref,
    key_hbm,
    value_hbm,
    out_weight_hbm,
    expert_gate_hbm,
    expert_up_hbm,
    expert_down_hbm,
    out_ref,
    key,
    value,
    out_weight,
    expert_gate,
    expert_up,
    expert_down,
    own,
    tok,
    y,
    y_own,
    y_send,
    y_recv,
    sum_send,
    sum_recv,
    qbuf,
    scores,
    parts,
    parts_in,
    hidden,
    dec_out,
    dec_in,
    ret_out,
    ret_in,
    load_sem,
    tok_send_sem,
    tok_recv_sem,
    sib_send_sem,
    sib_recv_sem,
    y_send_sem,
    y_recv_sem,
    sum_send_sem,
    sum_recv_sem,
    q_sems,
    p_sems,
    d_sems,
    r_sems,
):
    chips = n // 2
    half_chips = chips // 2
    me = lax.axis_index("kv")
    core = me % 2
    chip = me // 2
    position = (1 - chip % 2) * (chip // 2) + (chip % 2) * (chips - 1 - chip // 2)

    def at_position(place):
        upper = place // half_chips
        return ((1 - upper) * 2 * place + upper * (2 * (chips - 1 - place) + 1)) * 2 + core

    right = at_position((position + 1) % chips)
    left = at_position((position + chips - 1) % chips)
    sibling = chip * 2 + 1 - core
    rows, width = own.shape
    half = rows // 2
    pieces = width // LANES

    loads = [
        pltpu.make_async_copy(a, b, load_sem.at[i])
        for i, (a, b) in enumerate(
            (
                (expert_gate_hbm, expert_gate),
                (expert_up_hbm, expert_up),
                (expert_down_hbm, expert_down),
                (key_hbm, key),
                (value_hbm, value),
                (out_weight_hbm, out_weight),
            )
        )
    ]
    for load in loads:
        load.start()

    barrier = pltpu.get_barrier_semaphore()

    def greet(k, _):
        pl.semaphore_signal(
            barrier, inc=1, device_id={"kv": (me + k) % n}, device_id_type=MESH
        )
        return 0

    lax.fori_loop(1, n, greet, 0)

    lane = lax.broadcasted_iota(jnp.int32, (rows, LANES), 1)
    row = lax.broadcasted_iota(jnp.int32, (rows, LANES), 0)
    gate_grid = jnp.zeros((rows, LANES), jnp.float32)
    for k in range(TOPK):
        gate_grid += jnp.where(ids_ref[:, k : k + 1] == lane % 64, gates_ref[:, k : k + 1], 0.0)
    dec_out[...] = jnp.zeros_like(dec_out)
    dec_out[pieces : pieces + 1, :] = gate_grid[rows - 1 : rows, :]
    gate_grid = jnp.where(row == rows - 1, 0.0, gate_grid)
    gate_high = gate_grid.astype(jnp.bfloat16).astype(jnp.float32)
    packed = jnp.where(lane < 64, gate_high, gate_grid - gate_high).astype(jnp.bfloat16)
    own[0 : rows - 1, :] = prefill_ref[...].astype(jnp.float32)
    own[rows - 1 : rows, :] = jnp.zeros((1, width), jnp.float32)
    for i in range(2):
        wide = own[i * half : (i + 1) * half, :]
        scale = lax.rsqrt(jnp.mean(wide * wide, axis=-1, keepdims=True) + 1e-06)
        tok[0, i, :, 0:width] = (wide * scale * gain_ref[...]).astype(jnp.bfloat16)
        tok[0, i, :, width : width + LANES] = packed[i * half : (i + 1) * half, :]
    qbuf[me] = query_ref[...]

    pl.semaphore_wait(barrier, n - 1)

    def exchange(source, target, sems):
        def copy(k):
            peer = (me + k) % n
            return pltpu.make_async_remote_copy(
                source(peer),
                target.at[me],
                sems.at[0, k],
                sems.at[1, me],
                device_id={"kv": peer},
                device_id_type=MESH,
            )

        def arrival(k):
            peer = (me + k) % n
            return pltpu.make_async_remote_copy(
                source(peer),
                target.at[peer],
                sems.at[0, k],
                sems.at[1, peer],
                device_id={"kv": peer},
                device_id_type=MESH,
            )

        def start():
            def one(k, _):
                copy(k).start()
                return 0

            lax.fori_loop(1, n, one, 0)

        def finish():
            def one(k, _):
                arrival(k).wait_recv()
                copy(k).wait_send()
                return 0

            lax.fori_loop(1, n, one, 0)

        return start, finish

    start_q, finish_q = exchange(lambda k: query_ref, qbuf, q_sems)
    start_p, finish_p = exchange(lambda k: parts.at[k, 0:QUERY_HEADS], parts_in, p_sems)
    start_d, finish_d = exchange(lambda k: dec_out, dec_in, d_sems)
    start_r, finish_r = exchange(lambda k: ret_out.at[k], ret_in, r_sems)

    def token_copy(s, way):
        return pltpu.make_async_remote_copy(
            tok.at[s, way],
            tok.at[s + 1, way],
            tok_send_sem.at[s, way],
            tok_recv_sem.at[s + 1, way],
            device_id={"kv": (right, left)[way]},
            device_id_type=MESH,
        )

    def sibling_copy(s):
        return pltpu.make_async_remote_copy(
            tok.at[s, 0:2],
            tok.at[s, 2:4],
            sib_send_sem.at[s],
            sib_recv_sem.at[s],
            device_id={"kv": sibling},
            device_id_type=MESH,
        )

    def y_copy(s):
        return pltpu.make_async_remote_copy(
            y_send.at[s % 2],
            y_recv.at[s],
            y_send_sem.at[s],
            y_recv_sem.at[s],
            device_id={"kv": sibling},
            device_id_type=MESH,
        )

    def sum_copy(s, way):
        return pltpu.make_async_remote_copy(
            sum_send.at[s % 2, way],
            sum_recv.at[s, way],
            sum_send_sem.at[s, way],
            sum_recv_sem.at[s, way],
            device_id={"kv": (right, left)[way]},
            device_id_type=MESH,
        )

    def attend():
        finish_q()
        loads[3].wait()
        loads[4].wait()
        columns = KEY_VALUE_HEADS * HEAD_WIDTH
        count = n * HEAD_ROWS
        spread = (
            lax.broadcasted_iota(jnp.int32, (LANES, columns), 0)
            == lax.broadcasted_iota(jnp.int32, (LANES, columns), 1) % HEAD_WIDTH
        ).astype(jnp.float32).astype(jnp.bfloat16)
        group = QUERY_HEADS // KEY_VALUE_HEADS
        head = lax.broadcasted_iota(jnp.int32, (count, columns), 0) % HEAD_ROWS
        column = lax.broadcasted_iota(jnp.int32, (count, columns), 1)
        belongs = head // group == column // HEAD_WIDTH
        queries = qbuf[...].reshape(count, LANES)
        queries = jnp.dot(queries, spread, preferred_element_type=jnp.float32)
        queries = jnp.where(belongs, queries * HEAD_WIDTH**-0.5, 0.0).astype(jnp.bfloat16)
        scores[...] = lax.dot_general(
            queries, key[...], (((1,), (1,)), ((), ())), preferred_element_type=jnp.float32
        )
        lanes = lax.broadcasted_iota(jnp.int32, (HEAD_ROWS, LANES), 1)
        heads = lax.broadcasted_iota(jnp.int32, (HEAD_ROWS, LANES), 0)

        def per_request(r, _):
            at = pl.ds(pl.multiple_of(r * HEAD_ROWS, HEAD_ROWS), HEAD_ROWS)
            allowed = bias_ref[r] > 0.5
            score = jnp.where(allowed, scores[at, :], lowest)
            top = jnp.max(score, axis=-1, keepdims=True)
            weight = jnp.where(allowed, jnp.exp(score - top), 0.0)
            weight = weight.astype(jnp.bfloat16).astype(jnp.float32)
            total = jnp.sum(weight, axis=-1, keepdims=True)
            scores[at, :] = weight
            parts[r] = jnp.where(lanes % 64 < 32, top, total)
            return 0

        lax.fori_loop(0, n, per_request, 0)
        out = jnp.dot(
            scores[...].astype(jnp.bfloat16), value[...], preferred_element_type=jnp.float32
        )
        out = jnp.where(belongs, out, 0.0)
        folded = out[:, 0:LANES]
        for j in range(1, columns // LANES):
            folded += out[:, j * LANES : (j + 1) * LANES]
        in_half = (heads // group) % 2 == lanes // 64
        parts[...] = jnp.where(in_half[None], folded.reshape(n, HEAD_ROWS, LANES), parts[...])
        parts_in[me] = parts[me, 0:QUERY_HEADS]
        start_p()

    def project():
        finish_p()
        loads[5].wait()
        group = QUERY_HEADS // KEY_VALUE_HEADS
        lanes = lax.broadcasted_iota(jnp.int32, (QUERY_HEADS, LANES), 1)
        heads = lax.broadcasted_iota(jnp.int32, (QUERY_HEADS, LANES), 0)
        in_half = (heads // group) % 2 == lanes // 64
        is_top = jnp.logical_not(in_half) & (lanes % 64 < 32)
        is_total = jnp.logical_not(in_half) & (lanes % 64 >= 32)
        every = parts_in[...]
        tops = jnp.max(jnp.where(is_top[None], every, -3e38), axis=-1, keepdims=True)
        totals = jnp.max(jnp.where(is_total[None], every, -1.0), axis=-1, keepdims=True)
        top = jnp.max(tops, axis=0)
        share = jnp.exp(tops - top[None])
        total = jnp.sum(share * totals, axis=0)
        out = jnp.sum(share * every, axis=0)
        sink = sink_ref[...]
        ceiling = jnp.maximum(top, sink)
        keep = jnp.exp(top - ceiling)
        attended = out * (keep / (total * keep + jnp.exp(sink - ceiling)))
        attended = jnp.where(in_half, attended, 0.0)
        attended = attended + pltpu.roll(attended, 64, 1)
        low = lax.broadcasted_iota(jnp.int32, (1, LANES), 1) < 64
        line = jnp.concatenate(
            [
                jnp.where(low, attended[2 * j : 2 * j + 1, :], attended[2 * j + 1 : 2 * j + 2, :])
                for j in range(QUERY_HEADS // 2)
            ],
            axis=1,
        )
        line = jnp.broadcast_to(line, (16, line.shape[1])).astype(jnp.bfloat16)
        projected = jnp.dot(line, out_weight[...], preferred_element_type=jnp.float32)
        stream = (decode_ref[...].astype(jnp.float32) + projected[0:1, :]).astype(jnp.bfloat16)
        stream = stream.astype(jnp.float32)
        hidden[...] = stream
        scale = lax.rsqrt(jnp.mean(stream * stream, axis=-1, keepdims=True) + 1e-06)
        normed = stream * scale * gain_ref[...]
        for j in range(pieces):
            dec_out[j : j + 1, :] = normed[:, j * LANES : (j + 1) * LANES]
        dec_in[me] = dec_out[...]
        start_d()

    def decode_expert():
        finish_d()
        x = jnp.concatenate([dec_in[:, j, :] for j in range(pieces)], axis=1).astype(jnp.bfloat16)
        lanes = lax.broadcasted_iota(jnp.int32, (n, LANES), 1)
        weight = jnp.sum(
            jnp.where(lanes == me, dec_in[:, pieces, :], 0.0), axis=-1, keepdims=True
        )
        h = silu_times(
            jnp.dot(x, expert_gate[...], preferred_element_type=jnp.float32),
            jnp.dot(x, expert_up[...], preferred_element_type=jnp.float32),
        )
        made = jnp.dot(h, expert_down[...], preferred_element_type=jnp.float32) * weight
        ret_out[...] = jnp.zeros_like(ret_out)
        for j in range(pieces):
            ret_out[:, j, :] = made[:, j * LANES : (j + 1) * LANES]
        ret_in[me] = ret_out[me]
        start_r()

    def step(s, _):
        @pl.when(s >= 1)
        def _():
            token_copy(s - 1, 0).wait_recv()
            token_copy(s - 1, 1).wait_recv()

        @pl.when(s < chips - 1)
        def _():
            token_copy(s, 0).start()
            token_copy(s, 1).start()

        sibling_copy(s).start()

        @pl.when(s == 0)
        def _():
            start_q()
            for load in loads[:3]:
                load.wait()

        sibling_copy(s).wait_recv()
        x = tok[s].reshape(4 * half, width + LANES)
        lanes = lax.broadcasted_iota(jnp.int32, (4 * half, LANES), 1)
        weight = jnp.sum(
            jnp.where(lanes % 64 == me, x[:, width:].astype(jnp.float32), 0.0),
            axis=-1,
            keepdims=True,
        )
        x = x[:, 0:width]
        h = silu_times(
            jnp.dot(x, expert_gate[...], preferred_element_type=jnp.float32),
            jnp.dot(x, expert_up[...], preferred_element_type=jnp.float32),
        )
        y[...] = jnp.dot(h, expert_down[...], preferred_element_type=jnp.float32) * weight

        @pl.when(s >= 2)
        def _():
            y_copy(s - 2).wait_send()

        y_send[s % 2] = y[rows : 2 * rows, :].astype(jnp.bfloat16)
        y_copy(s).start()

        @pl.when(s == 1)
        def _():
            attend()

        @pl.when(s == chips // 2 - 1)
        def _():
            project()

        @pl.when(s == chips // 2 + 1)
        def _():
            decode_expert()

        y_copy(s).wait_recv()
        summed = y[0:rows, :] + y_recv[s].astype(jnp.float32)

        @pl.when(s == 0)
        def _():
            y_own[...] = summed

        @pl.when(s >= 1)
        def _():
            y[0:rows, :] = summed

        @pl.when(s >= 2)
        def _():
            for way in range(2):
                sum_copy(s - 1, way).wait_recv()
                at = slice(way * half, (way + 1) * half)
                y[at, :] = y[at, :] + sum_recv[s - 1, way].astype(jnp.float32)

        @pl.when(s >= 3)
        def _():
            sum_copy(s - 2, 0).wait_send()
            sum_copy(s - 2, 1).wait_send()

        @pl.when(s >= 1)
        def _():
            for way in range(2):
                at = slice(way * half, (way + 1) * half)
                sum_send[s % 2, way] = y[at, :].astype(jnp.bfloat16)
                sum_copy(s, way).start()

        return 0

    lax.fori_loop(0, chips, step, 0)

    last = chips - 1
    finish_r()
    line = jnp.sum(ret_in[...], axis=0)
    line = jnp.concatenate([line[j : j + 1, :] for j in range(pieces)], axis=1)
    line = line + hidden[...]
    for way in range(2):
        sum_copy(last, way).wait_recv()
        at = slice(way * half, (way + 1) * half)
        made = own[at, :] + y_own[at, :] + sum_recv[last, way].astype(jnp.float32)
        if way == 1:
            place = lax.broadcasted_iota(jnp.int32, (half, width), 0)
            made = jnp.where(place == half - 1, line, made)
        out_ref[at, :] = made.astype(jnp.bfloat16)

    def drain(s, _):
        token_copy(s, 0).wait_send()
        token_copy(s, 1).wait_send()
        return 0

    lax.fori_loop(0, chips - 1, drain, 0)

    def drain_sibling(s, _):
        sibling_copy(s).wait_send()
        return 0

    lax.fori_loop(0, chips, drain_sibling, 0)
    for s in (last - 1, last):
        y_copy(s).wait_send()
        for way in range(2):
            sum_copy(s, way).wait_send()


def on_device(
    queries,
    key_cache_pages,
    value_cache_pages,
    page_table,
    lengths,
    sink_head_logits,
    output_weight,
    decode_stream,
    prefill_stream,
    norm_gain,
    expert_gate,
    expert_up,
    expert_down,
    route_ids,
    route_gates,
):
    n = lax.axis_size("kv")
    chips = n // 2
    device_index = lax.axis_index(("ep", "kv"))
    pool, page_length, columns = key_cache_pages.shape
    rows = route_ids.shape[0]
    half = rows // 2
    width = prefill_stream.shape[1]
    hidden_units = expert_gate.shape[2]
    first = lax.axis_index("ep") * n
    table = lax.dynamic_slice_in_dim(page_table, first, n, 0)
    length = lax.dynamic_slice_in_dim(lengths, first, n, 0)
    begin = jnp.maximum(length - WINDOW, 0)
    first_page = begin // page_length
    slot = first_page[:, None] + jnp.arange(page_table.shape[1], dtype=jnp.int32)[None, :]
    live = slot * page_length < length[:, None]
    local = jnp.where(live, table - device_index * pool, -1)
    hit = local[:, None, :] == jnp.arange(pool, dtype=jnp.int32)[None, :, None]
    page = jnp.max(jnp.where(hit, slot[:, None, :], -1), axis=-1)
    where = page[:, :, None] * page_length + jnp.arange(page_length, dtype=jnp.int32)
    inside = (where >= begin[:, None, None]) & (where < length[:, None, None]) & (where >= 0)
    allowed = inside.astype(jnp.float32).reshape(n, 1, pool * page_length)
    query = jnp.pad(
        queries.reshape(QUERY_HEADS, HEAD_WIDTH),
        ((0, HEAD_ROWS - QUERY_HEADS), (0, LANES - HEAD_WIDTH)),
    )
    bf16, f32 = jnp.bfloat16, jnp.float32
    vmem = pl.BlockSpec(memory_space=pltpu.VMEM)
    hbm = pl.BlockSpec(memory_space=pl.ANY)
    dma = pltpu.SemaphoreType.DMA
    return pl.pallas_call(
        functools.partial(kernel, n),
        out_shape=jax.ShapeDtypeStruct((rows, width), bf16),
        in_specs=[vmem] * 8 + [hbm] * 6,
        out_specs=vmem,
        scratch_shapes=[
            pltpu.VMEM((pool * page_length, columns), bf16),
            pltpu.VMEM((pool * page_length, columns), bf16),
            pltpu.VMEM(output_weight.shape, bf16),
            pltpu.VMEM((width, hidden_units), bf16),
            pltpu.VMEM((width, hidden_units), bf16),
            pltpu.VMEM((hidden_units, width), bf16),
            pltpu.VMEM((rows, width), f32),
            pltpu.VMEM((chips, 4, half, width + LANES), bf16),
            pltpu.VMEM((2 * rows, width), f32),
            pltpu.VMEM((rows, width), f32),
            pltpu.VMEM((2, rows, width), bf16),
            pltpu.VMEM((chips, rows, width), bf16),
            pltpu.VMEM((2, 2, half, width), bf16),
            pltpu.VMEM((chips, 2, half, width), bf16),
            pltpu.VMEM((n, HEAD_ROWS, LANES), bf16),
            pltpu.VMEM((n * HEAD_ROWS, pool * page_length), f32),
            pltpu.VMEM((n, HEAD_ROWS, LANES), f32),
            pltpu.VMEM((n, QUERY_HEADS, LANES), f32),
            pltpu.VMEM((1, width), f32),
            pltpu.VMEM((16, LANES), f32),
            pltpu.VMEM((n, 16, LANES), f32),
            pltpu.VMEM((n, 16, LANES), f32),
            pltpu.VMEM((n, 16, LANES), f32),
            dma((6,)),
            dma((chips, 2)),
            dma((chips, 2)),
            dma((chips,)),
            dma((chips,)),
            dma((chips,)),
            dma((chips,)),
            dma((chips, 2)),
            dma((chips, 2)),
            dma((2, n)),
            dma((2, n)),
            dma((2, n)),
            dma((2, n)),
        ],
        compiler_params=pltpu.CompilerParams(
            collective_id=0, has_side_effects=True, vmem_limit_bytes=60 * 1024 * 1024
        ),
    )(
        query,
        allowed,
        sink_head_logits[:, None],
        decode_stream,
        prefill_stream,
        norm_gain[None, :],
        route_ids,
        route_gates,
        key_cache_pages.reshape(pool * page_length, columns),
        value_cache_pages.reshape(pool * page_length, columns),
        output_weight,
        expert_gate[0],
        expert_up[0],
        expert_down[0],
    )


def solution(mesh):
    in_specs = (
        P(("ep", "kv"), None),
        P(("ep", "kv"), None, None),
        P(("ep", "kv"), None, None),
        P(),
        P(),
        P(),
        P(),
        P(("ep", "kv"), None),
        P(("ep", "kv"), None),
        P(),
        P("kv", None, None),
        P("kv", None, None),
        P("kv", None, None),
        P(("ep", "kv"), None),
        P(("ep", "kv"), None),
    )
    out_specs = P(("ep", "kv"), None)
    return jax.shard_map(
        on_device, mesh=mesh, in_specs=in_specs, out_specs=out_specs, check_vma=False
    )
```

```python
import functools

import jax
import jax.numpy as jnp
from jax import lax
from jax.experimental import pallas as pl
from jax.experimental.pallas import tpu as pltpu
from jax.sharding import PartitionSpec as P

QUERY_HEADS = 24
KEY_VALUE_HEADS = 8
HEAD_WIDTH = 64
TOPK = 8
WINDOW = 4096
LANES = 128
HEAD_ROWS = 32

lowest = -1e30
MESH = pl.DeviceIdType.MESH


def silu_times(gate_part, up_part):
    return (gate_part / (1.0 + jnp.exp(-gate_part)) * up_part).astype(jnp.bfloat16)


def kernel(
    n,
    page_length,
    query_ref,
    table_ref,
    length_ref,
    sink_ref,
    decode_ref,
    prefill_ref,
    gain_ref,
    ids_ref,
    gates_ref,
    key_hbm,
    value_hbm,
    out_weight_hbm,
    expert_gate_hbm,
    expert_up_hbm,
    expert_down_hbm,
    out_ref,
    key,
    value,
    out_weight,
    expert_gate,
    expert_up,
    expert_down,
    own,
    tok,
    y,
    y_own,
    y_send,
    y_recv,
    sum_send,
    sum_recv,
    qown,
    bias,
    qbuf,
    scores,
    parts,
    parts_in,
    hidden,
    dec_out,
    dec_in,
    ret_out,
    ret_in,
    load_sem,
    tok_send_sem,
    tok_recv_sem,
    sib_send_sem,
    sib_recv_sem,
    y_send_sem,
    y_recv_sem,
    sum_send_sem,
    sum_recv_sem,
    q_sems,
    p_sems,
    d_sems,
    r_sems,
):
    chips = n // 2
    half_chips = chips // 2
    me = lax.axis_index("kv")
    core = me % 2
    chip = me // 2
    position = (1 - chip % 2) * (chip // 2) + (chip % 2) * (chips - 1 - chip // 2)

    def at_position(place):
        upper = place // half_chips
        return ((1 - upper) * 2 * place + upper * (2 * (chips - 1 - place) + 1)) * 2 + core

    right = at_position((position + 1) % chips)
    left = at_position((position + chips - 1) % chips)
    sibling = chip * 2 + 1 - core
    rows, width = own.shape
    half = rows // 2
    pieces = width // LANES

    loads = [
        pltpu.make_async_copy(a, b, load_sem.at[i])
        for i, (a, b) in enumerate(
            (
                (expert_gate_hbm, expert_gate),
                (expert_up_hbm, expert_up),
                (expert_down_hbm, expert_down),
                (key_hbm, key),
                (value_hbm, value),
                (out_weight_hbm, out_weight),
            )
        )
    ]
    for load in loads:
        load.start()

    barrier = pltpu.get_barrier_semaphore()

    def greet(k, _):
        pl.semaphore_signal(
            barrier, inc=1, device_id={"kv": (me + k) % n}, device_id_type=MESH
        )
        return 0

    lax.fori_loop(1, n, greet, 0)

    lane = lax.broadcasted_iota(jnp.int32, (rows, LANES), 1)
    row = lax.broadcasted_iota(jnp.int32, (rows, LANES), 0)
    expert_row = lax.broadcasted_iota(jnp.int32, (LANES, rows), 0) % 64
    gate_grid = jnp.zeros((LANES, rows), jnp.float32)
    for k in range(TOPK):
        gate_grid += jnp.where(ids_ref[k : k + 1, :] == expert_row, gates_ref[k : k + 1, :], 0.0)
    gate_grid = gate_grid.T
    gain = jnp.concatenate([gain_ref[j : j + 1, :] for j in range(pieces)], axis=1)
    dec_out[...] = jnp.zeros_like(dec_out)
    dec_out[pieces : pieces + 1, :] = gate_grid[rows - 1 : rows, :]
    gate_grid = jnp.where(row == rows - 1, 0.0, gate_grid)
    gate_high = gate_grid.astype(jnp.bfloat16).astype(jnp.float32)
    packed = jnp.where(lane < 64, gate_high, gate_grid - gate_high).astype(jnp.bfloat16)
    own[0 : rows - 1, :] = prefill_ref[...].astype(jnp.float32)
    own[rows - 1 : rows, :] = jnp.zeros((1, width), jnp.float32)
    for i in range(2):
        wide = own[i * half : (i + 1) * half, :]
        scale = lax.rsqrt(jnp.mean(wide * wide, axis=-1, keepdims=True) + 1e-06)
        tok[0, i, :, 0:width] = (wide * scale * gain).astype(jnp.bfloat16)
        tok[0, i, :, width : width + LANES] = packed[i * half : (i + 1) * half, :]
    wide_query = query_ref[...].astype(jnp.float32)
    for h in range(QUERY_HEADS):
        line = wide_query[:, h // 2 * LANES : h // 2 * LANES + LANES]
        qown_row = pltpu.roll(line, 64, 1) if h % 2 else line
        scores[h : h + 1, 0:LANES] = qown_row
    scores[QUERY_HEADS:HEAD_ROWS, 0:LANES] = jnp.zeros(
        (HEAD_ROWS - QUERY_HEADS, LANES), jnp.float32
    )
    qown[...] = scores[0:HEAD_ROWS, 0:LANES].astype(jnp.bfloat16)
    qbuf[me] = qown[...]

    pl.semaphore_wait(barrier, n - 1)

    def exchange(source, target, sems):
        def copy(k):
            peer = (me + k) % n
            return pltpu.make_async_remote_copy(
                source(peer),
                target.at[me],
                sems.at[0, k],
                sems.at[1, me],
                device_id={"kv": peer},
                device_id_type=MESH,
            )

        def arrival(k):
            peer = (me + k) % n
            return pltpu.make_async_remote_copy(
                source(peer),
                target.at[peer],
                sems.at[0, k],
                sems.at[1, peer],
                device_id={"kv": peer},
                device_id_type=MESH,
            )

        def start():
            def one(k, _):
                copy(k).start()
                return 0

            lax.fori_loop(1, n, one, 0)

        def finish():
            def one(k, _):
                arrival(k).wait_recv()
                copy(k).wait_send()
                return 0

            lax.fori_loop(1, n, one, 0)

        return start, finish

    start_q, finish_q = exchange(lambda k: qown, qbuf, q_sems)
    start_p, finish_p = exchange(lambda k: parts.at[k, 0:QUERY_HEADS], parts_in, p_sems)
    start_d, finish_d = exchange(lambda k: dec_out, dec_in, d_sems)
    start_r, finish_r = exchange(lambda k: ret_out.at[k], ret_in, r_sems)

    def token_copy(s, way):
        return pltpu.make_async_remote_copy(
            tok.at[s, way],
            tok.at[s + 1, way],
            tok_send_sem.at[s, way],
            tok_recv_sem.at[s + 1, way],
            device_id={"kv": (right, left)[way]},
            device_id_type=MESH,
        )

    def sibling_copy(s):
        return pltpu.make_async_remote_copy(
            tok.at[s, 0:2],
            tok.at[s, 2:4],
            sib_send_sem.at[s],
            sib_recv_sem.at[s],
            device_id={"kv": sibling},
            device_id_type=MESH,
        )

    def y_copy(s):
        return pltpu.make_async_remote_copy(
            y_send.at[s % 2],
            y_recv.at[s],
            y_send_sem.at[s],
            y_recv_sem.at[s],
            device_id={"kv": sibling},
            device_id_type=MESH,
        )

    def sum_copy(s, way):
        return pltpu.make_async_remote_copy(
            sum_send.at[s % 2, way],
            sum_recv.at[s, way],
            sum_send_sem.at[s, way],
            sum_recv_sem.at[s, way],
            device_id={"kv": (right, left)[way]},
            device_id_type=MESH,
        )

    def window_mask():
        requests, slots = table_ref.shape
        first = lax.axis_index("ep") * n
        pool = key.shape[0] // page_length
        across = lax.broadcasted_iota(jnp.int32, (n, requests), 1)
        down = lax.broadcasted_iota(jnp.int32, (n, requests), 0)
        length = jnp.sum(
            jnp.where(across == first + down, length_ref[...], 0), axis=-1, keepdims=True
        )
        begin = jnp.maximum(length - WINDOW, 0)
        slot = begin // page_length + lax.broadcasted_iota(jnp.int32, (n, slots), 1)
        table = table_ref[pl.ds(pl.multiple_of(first, 8), n), :]
        local = jnp.where(slot * page_length < length, table - (first + me) * pool, -1)
        lanes = lax.broadcasted_iota(jnp.int32, (n, LANES), 1)
        per = LANES // page_length
        for j in range(pool // per):
            page = jnp.full((n, LANES), -1, jnp.int32)
            for i in range(per):
                hit = jnp.where(local == j * per + i, slot, -1)
                held = jnp.max(hit, axis=-1, keepdims=True)
                page = jnp.where(lanes // page_length == i, held, page)
            place = page * page_length + lanes % page_length
            inside = (page >= 0) & (place >= begin) & (place < length)
            bias[:, j * LANES : (j + 1) * LANES] = jnp.where(inside, 1.0, 0.0)

    def attend():
        window_mask()
        finish_q()
        loads[3].wait()
        loads[4].wait()
        columns = KEY_VALUE_HEADS * HEAD_WIDTH
        count = n * HEAD_ROWS
        spread = (
            lax.broadcasted_iota(jnp.int32, (LANES, columns), 0)
            == lax.broadcasted_iota(jnp.int32, (LANES, columns), 1) % HEAD_WIDTH
        ).astype(jnp.float32).astype(jnp.bfloat16)
        group = QUERY_HEADS // KEY_VALUE_HEADS
        head = lax.broadcasted_iota(jnp.int32, (count, columns), 0) % HEAD_ROWS
        column = lax.broadcasted_iota(jnp.int32, (count, columns), 1)
        belongs = head // group == column // HEAD_WIDTH
        queries = qbuf[...].reshape(count, LANES)
        queries = jnp.dot(queries, spread, preferred_element_type=jnp.float32)
        queries = jnp.where(belongs, queries * HEAD_WIDTH**-0.5, 0.0).astype(jnp.bfloat16)
        scores[...] = lax.dot_general(
            queries, key[...], (((1,), (1,)), ((), ())), preferred_element_type=jnp.float32
        )
        lanes = lax.broadcasted_iota(jnp.int32, (HEAD_ROWS, LANES), 1)
        heads = lax.broadcasted_iota(jnp.int32, (HEAD_ROWS, LANES), 0)

        def per_request(r, _):
            at = pl.ds(pl.multiple_of(r * HEAD_ROWS, HEAD_ROWS), HEAD_ROWS)
            allowed = bias[pl.ds(r, 1), :] > 0.5
            score = jnp.where(allowed, scores[at, :], lowest)
            top = jnp.max(score, axis=-1, keepdims=True)
            weight = jnp.where(allowed, jnp.exp(score - top), 0.0)
            weight = weight.astype(jnp.bfloat16).astype(jnp.float32)
            total = jnp.sum(weight, axis=-1, keepdims=True)
            scores[at, :] = weight
            parts[r] = jnp.where(lanes % 64 < 32, top, total)
            return 0

        lax.fori_loop(0, n, per_request, 0)
        out = jnp.dot(
            scores[...].astype(jnp.bfloat16), value[...], preferred_element_type=jnp.float32
        )
        out = jnp.where(belongs, out, 0.0)
        folded = out[:, 0:LANES]
        for j in range(1, columns // LANES):
            folded += out[:, j * LANES : (j + 1) * LANES]
        in_half = (heads // group) % 2 == lanes // 64
        parts[...] = jnp.where(in_half[None], folded.reshape(n, HEAD_ROWS, LANES), parts[...])
        parts_in[me] = parts[me, 0:QUERY_HEADS]
        start_p()

    def project():
        finish_p()
        loads[5].wait()
        group = QUERY_HEADS // KEY_VALUE_HEADS
        lanes = lax.broadcasted_iota(jnp.int32, (QUERY_HEADS, LANES), 1)
        heads = lax.broadcasted_iota(jnp.int32, (QUERY_HEADS, LANES), 0)
        in_half = (heads // group) % 2 == lanes // 64
        is_top = jnp.logical_not(in_half) & (lanes % 64 < 32)
        is_total = jnp.logical_not(in_half) & (lanes % 64 >= 32)
        every = parts_in[...]
        tops = jnp.max(jnp.where(is_top[None], every, -3e38), axis=-1, keepdims=True)
        totals = jnp.max(jnp.where(is_total[None], every, -1.0), axis=-1, keepdims=True)
        top = jnp.max(tops, axis=0)
        share = jnp.exp(tops - top[None])
        total = jnp.sum(share * totals, axis=0)
        out = jnp.sum(share * every, axis=0)
        across = lax.broadcasted_iota(jnp.int32, (QUERY_HEADS, QUERY_HEADS), 1)
        down = lax.broadcasted_iota(jnp.int32, (QUERY_HEADS, QUERY_HEADS), 0)
        sink = jnp.sum(jnp.where(across == down, sink_ref[...], 0.0), axis=-1, keepdims=True)
        ceiling = jnp.maximum(top, sink)
        keep = jnp.exp(top - ceiling)
        attended = out * (keep / (total * keep + jnp.exp(sink - ceiling)))
        attended = jnp.where(in_half, attended, 0.0)
        attended = attended + pltpu.roll(attended, 64, 1)
        low = lax.broadcasted_iota(jnp.int32, (1, LANES), 1) < 64
        line = jnp.concatenate(
            [
                jnp.where(low, attended[2 * j : 2 * j + 1, :], attended[2 * j + 1 : 2 * j + 2, :])
                for j in range(QUERY_HEADS // 2)
            ],
            axis=1,
        )
        line = jnp.broadcast_to(line, (16, line.shape[1])).astype(jnp.bfloat16)
        projected = jnp.dot(line, out_weight[...], preferred_element_type=jnp.float32)
        stream = (decode_ref[...].astype(jnp.float32) + projected[0:1, :]).astype(jnp.bfloat16)
        stream = stream.astype(jnp.float32)
        hidden[...] = stream
        scale = lax.rsqrt(jnp.mean(stream * stream, axis=-1, keepdims=True) + 1e-06)
        normed = stream * scale * gain
        for j in range(pieces):
            dec_out[j : j + 1, :] = normed[:, j * LANES : (j + 1) * LANES]
        dec_in[me] = dec_out[...]
        start_d()

    def decode_expert():
        finish_d()
        x = jnp.concatenate([dec_in[:, j, :] for j in range(pieces)], axis=1).astype(jnp.bfloat16)
        lanes = lax.broadcasted_iota(jnp.int32, (n, LANES), 1)
        weight = jnp.sum(
            jnp.where(lanes == me, dec_in[:, pieces, :], 0.0), axis=-1, keepdims=True
        )
        h = silu_times(
            jnp.dot(x, expert_gate[...], preferred_element_type=jnp.float32),
            jnp.dot(x, expert_up[...], preferred_element_type=jnp.float32),
        )
        made = jnp.dot(h, expert_down[...], preferred_element_type=jnp.float32) * weight
        ret_out[...] = jnp.zeros_like(ret_out)
        for j in range(pieces):
            ret_out[:, j, :] = made[:, j * LANES : (j + 1) * LANES]
        ret_in[me] = ret_out[me]
        start_r()

    def step(s, _):
        @pl.when((s < chips - 1) & (s > 0))
        def _():
            token_copy(s, 0).wait_recv()
            token_copy(s, 1).wait_recv()

            @pl.when(s < chips - 2)
            def _():
                token_copy(s + 1, 0).start()
                token_copy(s + 1, 1).start()

            sibling_copy(s + 1).start()

        sibling_copy(s).wait_recv()
        x = tok[s].reshape(4 * half, width + LANES)
        lanes = lax.broadcasted_iota(jnp.int32, (4 * half, LANES), 1)
        weight = jnp.sum(
            jnp.where(lanes % 64 == me, x[:, width:].astype(jnp.float32), 0.0),
            axis=-1,
            keepdims=True,
        )
        x = x[:, 0:width]
        h = silu_times(
            jnp.dot(x, expert_gate[...], preferred_element_type=jnp.float32),
            jnp.dot(x, expert_up[...], preferred_element_type=jnp.float32),
        )
        y[...] = jnp.dot(h, expert_down[...], preferred_element_type=jnp.float32) * weight

        @pl.when(s >= 2)
        def _():
            y_copy(s - 2).wait_send()

        y_send[s % 2] = y[rows : 2 * rows, :].astype(jnp.bfloat16)
        y_copy(s).start()

        @pl.when(s == 0)
        def _():
            token_copy(s, 0).wait_recv()
            token_copy(s, 1).wait_recv()

            @pl.when(s < chips - 2)
            def _():
                token_copy(s + 1, 0).start()
                token_copy(s + 1, 1).start()

            sibling_copy(s + 1).start()

        @pl.when(s == 0)
        def _():
            attend()

        @pl.when(s == chips // 4)
        def _():
            project()

        @pl.when(s == chips // 2)
        def _():
            decode_expert()

        y_copy(s).wait_recv()
        summed = y[0:rows, :] + y_recv[s].astype(jnp.float32)

        @pl.when(s == 0)
        def _():
            y_own[...] = summed

        @pl.when(s >= 1)
        def _():
            y[0:rows, :] = summed

        @pl.when(s >= 2)
        def _():
            for way in range(2):
                sum_copy(s - 1, way).wait_recv()
                at = slice(way * half, (way + 1) * half)
                y[at, :] = y[at, :] + sum_recv[s - 1, way].astype(jnp.float32)

        @pl.when(s >= 3)
        def _():
            sum_copy(s - 2, 0).wait_send()
            sum_copy(s - 2, 1).wait_send()

        @pl.when(s >= 1)
        def _():
            for way in range(2):
                at = slice(way * half, (way + 1) * half)
                sum_send[s % 2, way] = y[at, :].astype(jnp.bfloat16)
                sum_copy(s, way).start()

        return 0

    for way in range(2):
        token_copy(0, way).start()
    sibling_copy(0).start()
    start_q()
    for load in loads[:3]:
        load.wait()
    lax.fori_loop(0, chips, step, 0)

    last = chips - 1
    finish_r()
    line = jnp.sum(ret_in[...], axis=0)
    line = jnp.concatenate([line[j : j + 1, :] for j in range(pieces)], axis=1)
    line = line + hidden[...]
    for way in range(2):
        sum_copy(last, way).wait_recv()
        at = slice(way * half, (way + 1) * half)
        made = own[at, :] + y_own[at, :] + sum_recv[last, way].astype(jnp.float32)
        if way == 1:
            place = lax.broadcasted_iota(jnp.int32, (half, width), 0)
            made = jnp.where(place == half - 1, line, made)
        out_ref[at, :] = made.astype(jnp.bfloat16)

    def drain(s, _):
        token_copy(s, 0).wait_send()
        token_copy(s, 1).wait_send()
        return 0

    lax.fori_loop(0, chips - 1, drain, 0)

    def drain_sibling(s, _):
        sibling_copy(s).wait_send()
        return 0

    lax.fori_loop(0, chips, drain_sibling, 0)
    for s in (last - 1, last):
        y_copy(s).wait_send()
        for way in range(2):
            sum_copy(s, way).wait_send()


def on_device(
    queries,
    key_cache_pages,
    value_cache_pages,
    page_table,
    lengths,
    sink_head_logits,
    output_weight,
    decode_stream,
    prefill_stream,
    norm_gain,
    expert_gate,
    expert_up,
    expert_down,
    route_ids,
    route_gates,
):
    n = lax.axis_size("kv")
    chips = n // 2
    pool, page_length, columns = key_cache_pages.shape
    rows = route_ids.shape[0]
    half = rows // 2
    width = prefill_stream.shape[1]
    hidden_units = expert_gate.shape[2]
    bf16, f32 = jnp.bfloat16, jnp.float32
    vmem = pl.BlockSpec(memory_space=pltpu.VMEM)
    hbm = pl.BlockSpec(memory_space=pl.ANY)
    dma = pltpu.SemaphoreType.DMA
    return pl.pallas_call(
        functools.partial(kernel, n, page_length),
        out_shape=jax.ShapeDtypeStruct((rows, width), bf16),
        in_specs=[vmem] * 9 + [hbm] * 6,
        out_specs=vmem,
        scratch_shapes=[
            pltpu.VMEM((pool * page_length, columns), bf16),
            pltpu.VMEM((pool * page_length, columns), bf16),
            pltpu.VMEM(output_weight.shape, bf16),
            pltpu.VMEM((width, hidden_units), bf16),
            pltpu.VMEM((width, hidden_units), bf16),
            pltpu.VMEM((hidden_units, width), bf16),
            pltpu.VMEM((rows, width), f32),
            pltpu.VMEM((chips, 4, half, width + LANES), bf16),
            pltpu.VMEM((2 * rows, width), f32),
            pltpu.VMEM((rows, width), f32),
            pltpu.VMEM((2, rows, width), bf16),
            pltpu.VMEM((chips, rows, width), bf16),
            pltpu.VMEM((2, 2, half, width), bf16),
            pltpu.VMEM((chips, 2, half, width), bf16),
            pltpu.VMEM((HEAD_ROWS, LANES), bf16),
            pltpu.VMEM((n, pool * page_length), f32),
            pltpu.VMEM((n, HEAD_ROWS, LANES), bf16),
            pltpu.VMEM((n * HEAD_ROWS, pool * page_length), f32),
            pltpu.VMEM((n, HEAD_ROWS, LANES), f32),
            pltpu.VMEM((n, QUERY_HEADS, LANES), f32),
            pltpu.VMEM((1, width), f32),
            pltpu.VMEM((16, LANES), f32),
            pltpu.VMEM((n, 16, LANES), f32),
            pltpu.VMEM((n, 16, LANES), f32),
            pltpu.VMEM((n, 16, LANES), f32),
            dma((6,)),
            dma((chips, 2)),
            dma((chips, 2)),
            dma((chips,)),
            dma((chips,)),
            dma((chips,)),
            dma((chips,)),
            dma((chips, 2)),
            dma((chips, 2)),
            dma((2, n)),
            dma((2, n)),
            dma((2, n)),
            dma((2, n)),
        ],
        compiler_params=pltpu.CompilerParams(
            collective_id=0, has_side_effects=True, vmem_limit_bytes=60 * 1024 * 1024
        ),
    )(
        queries,
        page_table,
        lengths[None, :],
        sink_head_logits[None, :],
        decode_stream,
        prefill_stream,
        norm_gain.reshape(width // LANES, LANES),
        route_ids.T,
        route_gates.T,
        key_cache_pages.reshape(pool * page_length, columns),
        value_cache_pages.reshape(pool * page_length, columns),
        output_weight,
        expert_gate[0],
        expert_up[0],
        expert_down[0],
    )


def solution(mesh):
    in_specs = (
        P(("ep", "kv"), None),
        P(("ep", "kv"), None, None),
        P(("ep", "kv"), None, None),
        P(),
        P(),
        P(),
        P(),
        P(("ep", "kv"), None),
        P(("ep", "kv"), None),
        P(),
        P("kv", None, None),
        P("kv", None, None),
        P("kv", None, None),
        P(("ep", "kv"), None),
        P(("ep", "kv"), None),
    )
    out_specs = P(("ep", "kv"), None)
    return jax.shard_map(
        on_device, mesh=mesh, in_specs=in_specs, out_specs=out_specs, check_vma=False
    )
```

```python
import functools

import jax
import jax.numpy as jnp
from jax import lax
from jax.experimental import pallas as pl
from jax.experimental.pallas import tpu as pltpu
from jax.sharding import PartitionSpec as P

QUERY_HEADS = 24
KEY_VALUE_HEADS = 8
HEAD_WIDTH = 64
TOPK = 8
WINDOW = 4096
LANES = 128
HEAD_ROWS = 32

lowest = -1e30
MESH = pl.DeviceIdType.MESH


def silu_times(gate_part, up_part):
    return (gate_part / (1.0 + jnp.exp(-gate_part)) * up_part).astype(jnp.bfloat16)


def kernel(
    n,
    page_length,
    query_ref,
    table_ref,
    length_ref,
    sink_ref,
    decode_ref,
    prefill_ref,
    gain_ref,
    ids_ref,
    gates_ref,
    key_hbm,
    value_hbm,
    out_weight_hbm,
    expert_gate_hbm,
    expert_up_hbm,
    expert_down_hbm,
    out_ref,
    key,
    value,
    out_weight,
    expert_gate,
    expert_up,
    expert_down,
    own,
    tok,
    y,
    y_own,
    y_send,
    y_recv,
    sum_send,
    sum_recv,
    qown,
    bias,
    qbuf,
    scores,
    parts,
    parts_in,
    hidden,
    dec_out,
    dec_in,
    ret_out,
    ret_in,
    load_sem,
    tok_send_sem,
    tok_recv_sem,
    sib_send_sem,
    sib_recv_sem,
    y_send_sem,
    y_recv_sem,
    sum_send_sem,
    sum_recv_sem,
    q_sems,
    p_sems,
    d_sems,
    r_sems,
):
    chips = n // 2
    half_chips = chips // 2
    me = lax.axis_index("kv")
    core = me % 2
    chip = me // 2
    position = (1 - chip % 2) * (chip // 2) + (chip % 2) * (chips - 1 - chip // 2)

    def at_position(place):
        upper = place // half_chips
        return ((1 - upper) * 2 * place + upper * (2 * (chips - 1 - place) + 1)) * 2 + core

    right = at_position((position + 1) % chips)
    left = at_position((position + chips - 1) % chips)
    sibling = chip * 2 + 1 - core
    rows, width = own.shape
    half = rows // 2
    pieces = width // LANES

    loads = [
        pltpu.make_async_copy(a, b, load_sem.at[i])
        for i, (a, b) in enumerate(
            (
                (expert_gate_hbm, expert_gate),
                (expert_up_hbm, expert_up),
                (expert_down_hbm, expert_down),
                (key_hbm, key),
                (value_hbm, value),
                (out_weight_hbm, out_weight),
            )
        )
    ]
    for load in loads:
        load.start()

    barrier = pltpu.get_barrier_semaphore()

    def greet(k, _):
        pl.semaphore_signal(
            barrier, inc=1, device_id={"kv": (me + k) % n}, device_id_type=MESH
        )
        return 0

    lax.fori_loop(1, n, greet, 0)

    lane = lax.broadcasted_iota(jnp.int32, (rows, LANES), 1)
    row = lax.broadcasted_iota(jnp.int32, (rows, LANES), 0)
    expert_row = lax.broadcasted_iota(jnp.int32, (LANES, rows), 0) % 64
    gate_grid = jnp.zeros((LANES, rows), jnp.float32)
    for k in range(TOPK):
        gate_grid += jnp.where(ids_ref[k : k + 1, :] == expert_row, gates_ref[k : k + 1, :], 0.0)
    gate_grid = gate_grid.T
    gain = jnp.concatenate([gain_ref[j : j + 1, :] for j in range(pieces)], axis=1)
    dec_out[...] = jnp.zeros_like(dec_out)
    dec_out[pieces : pieces + 1, :] = gate_grid[rows - 1 : rows, :]
    gate_grid = jnp.where(row == rows - 1, 0.0, gate_grid)
    gate_high = gate_grid.astype(jnp.bfloat16).astype(jnp.float32)
    packed = jnp.where(lane < 64, gate_high, gate_grid - gate_high).astype(jnp.bfloat16)
    own[0 : rows - 1, :] = prefill_ref[...].astype(jnp.float32)
    own[rows - 1 : rows, :] = jnp.zeros((1, width), jnp.float32)
    for i in range(2):
        wide = own[i * half : (i + 1) * half, :]
        scale = lax.rsqrt(jnp.mean(wide * wide, axis=-1, keepdims=True) + 1e-06)
        tok[0, i, :, 0:width] = (wide * scale * gain).astype(jnp.bfloat16)
        tok[0, i, :, width : width + LANES] = packed[i * half : (i + 1) * half, :]
    wide_query = query_ref[...].astype(jnp.float32)
    for h in range(QUERY_HEADS):
        line = wide_query[:, h // 2 * LANES : h // 2 * LANES + LANES]
        qown_row = pltpu.roll(line, 64, 1) if h % 2 else line
        scores[h : h + 1, 0:LANES] = qown_row
    scores[QUERY_HEADS:HEAD_ROWS, 0:LANES] = jnp.zeros(
        (HEAD_ROWS - QUERY_HEADS, LANES), jnp.float32
    )
    qown[...] = scores[0:HEAD_ROWS, 0:LANES].astype(jnp.bfloat16)
    qbuf[me] = qown[...]

    pl.semaphore_wait(barrier, n - 1)

    def exchange(source, target, sems):
        def copy(k):
            peer = (me + k) % n
            return pltpu.make_async_remote_copy(
                source(peer),
                target.at[me],
                sems.at[0, k],
                sems.at[1, me],
                device_id={"kv": peer},
                device_id_type=MESH,
            )

        def arrival(k):
            peer = (me + k) % n
            return pltpu.make_async_remote_copy(
                source(peer),
                target.at[peer],
                sems.at[0, k],
                sems.at[1, peer],
                device_id={"kv": peer},
                device_id_type=MESH,
            )

        def start():
            def one(k, _):
                copy(k).start()
                return 0

            lax.fori_loop(1, n, one, 0)

        def finish():
            def one(k, _):
                arrival(k).wait_recv()
                copy(k).wait_send()
                return 0

            lax.fori_loop(1, n, one, 0)

        return start, finish

    start_q, finish_q = exchange(lambda k: qown, qbuf, q_sems)
    start_p, finish_p = exchange(lambda k: parts.at[k, 0:QUERY_HEADS], parts_in, p_sems)
    start_d, finish_d = exchange(lambda k: dec_out, dec_in, d_sems)
    start_r, finish_r = exchange(lambda k: ret_out.at[k], ret_in, r_sems)

    def token_copy(s, way):
        return pltpu.make_async_remote_copy(
            tok.at[s, way],
            tok.at[s + 1, way],
            tok_send_sem.at[s, way],
            tok_recv_sem.at[s + 1, way],
            device_id={"kv": (right, left)[way]},
            device_id_type=MESH,
        )

    def sibling_copy(s):
        return pltpu.make_async_remote_copy(
            tok.at[s, 0:2],
            tok.at[s, 2:4],
            sib_send_sem.at[s],
            sib_recv_sem.at[s],
            device_id={"kv": sibling},
            device_id_type=MESH,
        )

    def y_copy(s):
        return pltpu.make_async_remote_copy(
            y_send.at[s % 2],
            y_recv.at[s],
            y_send_sem.at[s],
            y_recv_sem.at[s],
            device_id={"kv": sibling},
            device_id_type=MESH,
        )

    def sum_copy(s, way):
        return pltpu.make_async_remote_copy(
            sum_send.at[s % 2, way],
            sum_recv.at[s, way],
            sum_send_sem.at[s, way],
            sum_recv_sem.at[s, way],
            device_id={"kv": (right, left)[way]},
            device_id_type=MESH,
        )

    def window_mask():
        requests, slots = table_ref.shape
        first = lax.axis_index("ep") * n
        pool = key.shape[0] // page_length
        across = lax.broadcasted_iota(jnp.int32, (n, requests), 1)
        down = lax.broadcasted_iota(jnp.int32, (n, requests), 0)
        length = jnp.sum(
            jnp.where(across == first + down, length_ref[...], 0), axis=-1, keepdims=True
        )
        begin = jnp.maximum(length - WINDOW, 0)
        slot = begin // page_length + lax.broadcasted_iota(jnp.int32, (n, slots), 1)
        table = table_ref[pl.ds(pl.multiple_of(first, 8), n), :]
        local = jnp.where(slot * page_length < length, table - (first + me) * pool, -1)
        lanes = lax.broadcasted_iota(jnp.int32, (n, LANES), 1)
        per = LANES // page_length
        for j in range(pool // per):
            page = jnp.full((n, LANES), -1, jnp.int32)
            for i in range(per):
                hit = jnp.where(local == j * per + i, slot, -1)
                held = jnp.max(hit, axis=-1, keepdims=True)
                page = jnp.where(lanes // page_length == i, held, page)
            place = page * page_length + lanes % page_length
            inside = (page >= 0) & (place >= begin) & (place < length)
            bias[:, j * LANES : (j + 1) * LANES] = jnp.where(inside, 1.0, 0.0)

    def attend():
        window_mask()
        finish_q()
        loads[3].wait()
        loads[4].wait()
        columns = KEY_VALUE_HEADS * HEAD_WIDTH
        count = n * HEAD_ROWS
        spread = (
            lax.broadcasted_iota(jnp.int32, (LANES, columns), 0)
            == lax.broadcasted_iota(jnp.int32, (LANES, columns), 1) % HEAD_WIDTH
        ).astype(jnp.float32).astype(jnp.bfloat16)
        group = QUERY_HEADS // KEY_VALUE_HEADS
        head = lax.broadcasted_iota(jnp.int32, (count, columns), 0) % HEAD_ROWS
        column = lax.broadcasted_iota(jnp.int32, (count, columns), 1)
        belongs = head // group == column // HEAD_WIDTH
        queries = qbuf[...].reshape(count, LANES)
        queries = jnp.dot(queries, spread, preferred_element_type=jnp.float32)
        queries = jnp.where(belongs, queries * HEAD_WIDTH**-0.5, 0.0).astype(jnp.bfloat16)
        scores[...] = lax.dot_general(
            queries, key[...], (((1,), (1,)), ((), ())), preferred_element_type=jnp.float32
        )
        lanes = lax.broadcasted_iota(jnp.int32, (HEAD_ROWS, LANES), 1)
        heads = lax.broadcasted_iota(jnp.int32, (HEAD_ROWS, LANES), 0)

        def per_request(r, _):
            at = pl.ds(pl.multiple_of(r * HEAD_ROWS, HEAD_ROWS), HEAD_ROWS)
            allowed = bias[pl.ds(r, 1), :] > 0.5
            score = jnp.where(allowed, scores[at, :], lowest)
            top = jnp.max(score, axis=-1, keepdims=True)
            weight = jnp.where(allowed, jnp.exp(score - top), 0.0)
            weight = weight.astype(jnp.bfloat16).astype(jnp.float32)
            total = jnp.sum(weight, axis=-1, keepdims=True)
            scores[at, :] = weight
            parts[r] = jnp.where(lanes % 64 < 32, top, total)
            return 0

        lax.fori_loop(0, n, per_request, 0)
        out = jnp.dot(
            scores[...].astype(jnp.bfloat16), value[...], preferred_element_type=jnp.float32
        )
        out = jnp.where(belongs, out, 0.0)
        folded = out[:, 0:LANES]
        for j in range(1, columns // LANES):
            folded += out[:, j * LANES : (j + 1) * LANES]
        in_half = (heads // group) % 2 == lanes // 64
        parts[...] = jnp.where(in_half[None], folded.reshape(n, HEAD_ROWS, LANES), parts[...])
        parts_in[me] = parts[me, 0:QUERY_HEADS]
        start_p()

    def project():
        finish_p()
        loads[5].wait()
        group = QUERY_HEADS // KEY_VALUE_HEADS
        lanes = lax.broadcasted_iota(jnp.int32, (QUERY_HEADS, LANES), 1)
        heads = lax.broadcasted_iota(jnp.int32, (QUERY_HEADS, LANES), 0)
        in_half = (heads // group) % 2 == lanes // 64
        is_top = jnp.logical_not(in_half) & (lanes % 64 < 32)
        is_total = jnp.logical_not(in_half) & (lanes % 64 >= 32)
        every = parts_in[...]
        tops = jnp.max(jnp.where(is_top[None], every, -3e38), axis=-1, keepdims=True)
        totals = jnp.max(jnp.where(is_total[None], every, -1.0), axis=-1, keepdims=True)
        top = jnp.max(tops, axis=0)
        share = jnp.exp(tops - top[None])
        total = jnp.sum(share * totals, axis=0)
        out = jnp.sum(share * every, axis=0)
        across = lax.broadcasted_iota(jnp.int32, (QUERY_HEADS, QUERY_HEADS), 1)
        down = lax.broadcasted_iota(jnp.int32, (QUERY_HEADS, QUERY_HEADS), 0)
        sink = jnp.sum(jnp.where(across == down, sink_ref[...], 0.0), axis=-1, keepdims=True)
        ceiling = jnp.maximum(top, sink)
        keep = jnp.exp(top - ceiling)
        attended = out * (keep / (total * keep + jnp.exp(sink - ceiling)))
        attended = jnp.where(in_half, attended, 0.0)
        attended = attended + pltpu.roll(attended, 64, 1)
        low = lax.broadcasted_iota(jnp.int32, (1, LANES), 1) < 64
        line = jnp.concatenate(
            [
                jnp.where(low, attended[2 * j : 2 * j + 1, :], attended[2 * j + 1 : 2 * j + 2, :])
                for j in range(QUERY_HEADS // 2)
            ],
            axis=1,
        )
        line = jnp.broadcast_to(line, (16, line.shape[1])).astype(jnp.bfloat16)
        projected = jnp.dot(line, out_weight[...], preferred_element_type=jnp.float32)
        stream = (decode_ref[...].astype(jnp.float32) + projected[0:1, :]).astype(jnp.bfloat16)
        stream = stream.astype(jnp.float32)
        hidden[...] = stream
        scale = lax.rsqrt(jnp.mean(stream * stream, axis=-1, keepdims=True) + 1e-06)
        normed = stream * scale * gain
        for j in range(pieces):
            dec_out[j : j + 1, :] = normed[:, j * LANES : (j + 1) * LANES]
        dec_in[me] = dec_out[...]
        start_d()

    def decode_expert():
        finish_d()
        x = jnp.concatenate([dec_in[:, j, :] for j in range(pieces)], axis=1).astype(jnp.bfloat16)
        lanes = lax.broadcasted_iota(jnp.int32, (n, LANES), 1)
        weight = jnp.sum(
            jnp.where(lanes == me, dec_in[:, pieces, :], 0.0), axis=-1, keepdims=True
        )
        h = silu_times(
            jnp.dot(x, expert_gate[...], preferred_element_type=jnp.float32),
            jnp.dot(x, expert_up[...], preferred_element_type=jnp.float32),
        )
        made = jnp.dot(h, expert_down[...], preferred_element_type=jnp.float32) * weight
        ret_out[...] = jnp.zeros_like(ret_out)
        for j in range(pieces):
            ret_out[:, j, :] = made[:, j * LANES : (j + 1) * LANES]
        ret_in[me] = ret_out[me]
        start_r()

    def step(s, _):
        @pl.when((s < chips - 1) & (s > 0))
        def _():
            token_copy(s, 0).wait_recv()
            token_copy(s, 1).wait_recv()

            @pl.when(s < chips - 2)
            def _():
                token_copy(s + 1, 0).start()
                token_copy(s + 1, 1).start()

            sibling_copy(s + 1).start()

        sibling_copy(s).wait_recv()
        x = tok[s].reshape(4 * half, width + LANES)
        lanes = lax.broadcasted_iota(jnp.int32, (4 * half, LANES), 1)
        weight = jnp.sum(
            jnp.where(lanes % 64 == me, x[:, width:].astype(jnp.float32), 0.0),
            axis=-1,
            keepdims=True,
        )
        x = x[:, 0:width]
        h = silu_times(
            jnp.dot(x, expert_gate[...], preferred_element_type=jnp.float32),
            jnp.dot(x, expert_up[...], preferred_element_type=jnp.float32),
        )
        y[...] = jnp.dot(h, expert_down[...], preferred_element_type=jnp.float32) * weight

        @pl.when(s >= 2)
        def _():
            y_copy(s - 2).wait_send()

        y_send[s % 2] = y[rows : 2 * rows, :].astype(jnp.bfloat16)
        y_copy(s).start()

        @pl.when(s == 0)
        def _():
            token_copy(s, 0).wait_recv()
            token_copy(s, 1).wait_recv()

            @pl.when(s < chips - 2)
            def _():
                token_copy(s + 1, 0).start()
                token_copy(s + 1, 1).start()

            sibling_copy(s + 1).start()

        @pl.when(s == 0)
        def _():
            attend()

        @pl.when(s == chips // 2 - 1)
        def _():
            project()

        @pl.when(s == chips - 2)
        def _():
            decode_expert()

        y_copy(s).wait_recv()
        summed = y[0:rows, :] + y_recv[s].astype(jnp.float32)

        @pl.when(s == 0)
        def _():
            y_own[...] = summed

        @pl.when(s >= 1)
        def _():
            y[0:rows, :] = summed

        @pl.when(s >= 2)
        def _():
            for way in range(2):
                sum_copy(s - 1, way).wait_recv()
                at = slice(way * half, (way + 1) * half)
                y[at, :] = y[at, :] + sum_recv[s - 1, way].astype(jnp.float32)

        @pl.when(s >= 3)
        def _():
            sum_copy(s - 2, 0).wait_send()
            sum_copy(s - 2, 1).wait_send()

        @pl.when(s >= 1)
        def _():
            for way in range(2):
                at = slice(way * half, (way + 1) * half)
                sum_send[s % 2, way] = y[at, :].astype(jnp.bfloat16)
                sum_copy(s, way).start()

        return 0

    start_q()
    for way in range(2):
        token_copy(0, way).start()
    sibling_copy(0).start()
    for load in loads[:3]:
        load.wait()
    lax.fori_loop(0, chips, step, 0)

    last = chips - 1
    finish_r()
    line = jnp.sum(ret_in[...], axis=0)
    line = jnp.concatenate([line[j : j + 1, :] for j in range(pieces)], axis=1)
    line = line + hidden[...]
    for way in range(2):
        sum_copy(last, way).wait_recv()
        at = slice(way * half, (way + 1) * half)
        made = own[at, :] + y_own[at, :] + sum_recv[last, way].astype(jnp.float32)
        if way == 1:
            place = lax.broadcasted_iota(jnp.int32, (half, width), 0)
            made = jnp.where(place == half - 1, line, made)
        out_ref[at, :] = made.astype(jnp.bfloat16)

    def drain(s, _):
        token_copy(s, 0).wait_send()
        token_copy(s, 1).wait_send()
        return 0

    lax.fori_loop(0, chips - 1, drain, 0)

    def drain_sibling(s, _):
        sibling_copy(s).wait_send()
        return 0

    lax.fori_loop(0, chips, drain_sibling, 0)
    for s in (last - 1, last):
        y_copy(s).wait_send()
        for way in range(2):
            sum_copy(s, way).wait_send()


def on_device(
    queries,
    key_cache_pages,
    value_cache_pages,
    page_table,
    lengths,
    sink_head_logits,
    output_weight,
    decode_stream,
    prefill_stream,
    norm_gain,
    expert_gate,
    expert_up,
    expert_down,
    route_ids,
    route_gates,
):
    n = lax.axis_size("kv")
    chips = n // 2
    pool, page_length, columns = key_cache_pages.shape
    rows = route_ids.shape[0]
    half = rows // 2
    width = prefill_stream.shape[1]
    hidden_units = expert_gate.shape[2]
    bf16, f32 = jnp.bfloat16, jnp.float32
    vmem = pl.BlockSpec(memory_space=pltpu.VMEM)
    hbm = pl.BlockSpec(memory_space=pl.ANY)
    dma = pltpu.SemaphoreType.DMA
    return pl.pallas_call(
        functools.partial(kernel, n, page_length),
        out_shape=jax.ShapeDtypeStruct((rows, width), bf16),
        in_specs=[vmem] * 9 + [hbm] * 6,
        out_specs=vmem,
        scratch_shapes=[
            pltpu.VMEM((pool * page_length, columns), bf16),
            pltpu.VMEM((pool * page_length, columns), bf16),
            pltpu.VMEM(output_weight.shape, bf16),
            pltpu.VMEM((width, hidden_units), bf16),
            pltpu.VMEM((width, hidden_units), bf16),
            pltpu.VMEM((hidden_units, width), bf16),
            pltpu.VMEM((rows, width), f32),
            pltpu.VMEM((chips, 4, half, width + LANES), bf16),
            pltpu.VMEM((2 * rows, width), f32),
            pltpu.VMEM((rows, width), f32),
            pltpu.VMEM((2, rows, width), bf16),
            pltpu.VMEM((chips, rows, width), bf16),
            pltpu.VMEM((2, 2, half, width), bf16),
            pltpu.VMEM((chips, 2, half, width), bf16),
            pltpu.VMEM((HEAD_ROWS, LANES), bf16),
            pltpu.VMEM((n, pool * page_length), f32),
            pltpu.VMEM((n, HEAD_ROWS, LANES), bf16),
            pltpu.VMEM((n * HEAD_ROWS, pool * page_length), f32),
            pltpu.VMEM((n, HEAD_ROWS, LANES), f32),
            pltpu.VMEM((n, QUERY_HEADS, LANES), f32),
            pltpu.VMEM((1, width), f32),
            pltpu.VMEM((16, LANES), f32),
            pltpu.VMEM((n, 16, LANES), f32),
            pltpu.VMEM((n, 16, LANES), f32),
            pltpu.VMEM((n, 16, LANES), f32),
            dma((6,)),
            dma((chips, 2)),
            dma((chips, 2)),
            dma((chips,)),
            dma((chips,)),
            dma((chips,)),
            dma((chips,)),
            dma((chips, 2)),
            dma((chips, 2)),
            dma((2, n)),
            dma((2, n)),
            dma((2, n)),
            dma((2, n)),
        ],
        compiler_params=pltpu.CompilerParams(
            collective_id=0, has_side_effects=True, vmem_limit_bytes=60 * 1024 * 1024
        ),
    )(
        queries,
        page_table,
        lengths[None, :],
        sink_head_logits[None, :],
        decode_stream,
        prefill_stream,
        norm_gain.reshape(width // LANES, LANES),
        route_ids.T,
        route_gates.T,
        key_cache_pages.reshape(pool * page_length, columns),
        value_cache_pages.reshape(pool * page_length, columns),
        output_weight,
        expert_gate[0],
        expert_up[0],
        expert_down[0],
    )


def solution(mesh):
    in_specs = (
        P(("ep", "kv"), None),
        P(("ep", "kv"), None, None),
        P(("ep", "kv"), None, None),
        P(),
        P(),
        P(),
        P(),
        P(("ep", "kv"), None),
        P(("ep", "kv"), None),
        P(),
        P("kv", None, None),
        P("kv", None, None),
        P("kv", None, None),
        P(("ep", "kv"), None),
        P(("ep", "kv"), None),
    )
    out_specs = P(("ep", "kv"), None)
    return jax.shard_map(
        on_device, mesh=mesh, in_specs=in_specs, out_specs=out_specs, check_vma=False
    )
```
